128 devices in a mesh: pipe: 8 (over y, z_lo), expert: 8 (over z_hi, x), dp: 2 (over core).
Axes of the slice: x: 4, y: 4, z: 4 (z_hi: 2, z_lo: 2; z = z_hi * 2 + z_lo), core: 2. Of those that a mesh axis runs over, the one named last changes fastest.
Arguments:
- rising_in: bfloat16 [8, 2048, 7168], P('pipe', ('expert', 'dp')), may hold values from -6 to 6
- rising_ids: int32 [8, 2048, 2], P('pipe', ('expert', 'dp')), may hold values from 0 to 7, all different within a row; in each aligned block of 128 rows (0 to 127, 128 to 255, ..., all dimensions but the last counted through in order) at most 40 rows name the same one
- rising_gates: float32 [8, 2048, 2], P('pipe', ('expert', 'dp')), may hold values from 0.1 to 1
- rising_drop: int32 [8, 2, 64], P('pipe', None, ('expert', 'dp')), may hold values from -2147483648 to 2147483647, as said below
- sinking_grad: bfloat16 [8, 2048, 7168], P('pipe', ('expert', 'dp')), may hold values from -6 to 6
- sinking_ids: int32 [8, 2048, 2], P('pipe', ('expert', 'dp')), may hold values from 0 to 7, all different within a row; in each aligned block of 128 rows (0 to 127, 128 to 255, ..., all dimensions but the last counted through in order) at most 40 rows name the same one
- sinking_gates: float32 [8, 2048, 2], P('pipe', ('expert', 'dp')), may hold values from 0.1 to 1
- sinking_drop: int32 [8, 2, 64], P('pipe', None, ('expert', 'dp')), may hold values from -2147483648 to 2147483647, as said below
- sinking_pre: bfloat16 [8, 8, 640, 1024], P('pipe', 'expert', None, 'dp'), may hold values from -6 to 6
- w_in: bfloat16 [8, 8, 7168, 1024], P('pipe', 'expert', None, 'dp'), may hold values from -0.0625 to 0.0625
- w_out: bfloat16 [8, 8, 1024, 7168], P('pipe', 'expert', 'dp'), may hold values from -0.1875 to 0.1875
Outputs:
- rising_out: bfloat16 [8, 2048, 7168], P('pipe', ('expert', 'dp'))
- sinking_out: bfloat16 [8, 2048, 7168], P('pipe', ('expert', 'dp'))
The draws below stay inside these ranges and needn't reach their ends.
Inputs may be any that keep to these rules, and one draw needn't show every extreme that they name: `rising_ids`: each token names 2 different experts; in each device's aligned block of 128 tokens of a section no expert is named by more than 40 tokens, a bound that some block reaches. `sinking_ids`: each token names 2 different experts; in each device's aligned block of 128 tokens of a section no expert is named by more than 40 tokens, a bound that some block reaches. `rising_drop`: all 32 bits of each word are used. `sinking_drop`: all 32 bits of each word are used.
All inputs are finite; a program needn't handle non-finite values.
Results may differ from the reference program's by a relative error of at most 0.0072.
Values may be sent and summed in bfloat16 or wider, within the bound.
A program may use at most 128 MiB of HBM per device.

```python
import math
import jax
import jax.numpy as jnp
import numpy as np
from jax import lax

D = 7168
HID = 1024
TOK_DEV = 128
TOP = 2
SECTIONS = 8
EXPERTS = 8
TOKENS = 2048
CAP = 40
SLOTS = 640
N_DP = 2


def packed_bits(key, shape):

    def add_bit(place, words):
        draw = jax.random.randint(jax.random.fold_in(key, place), shape, 0, 10)
        return words | jnp.where(draw < 9, jnp.left_shift(jnp.int32(1), place), jnp.int32(0))
    return lax.fori_loop(0, 32, add_bit, jnp.zeros(shape, jnp.int32))


def draw_rising_drop(key, part):
    key = jax.random.fold_in(key, 11)
    return packed_bits(key, (SECTIONS, TOP, TOKENS // 32))


def draw_sinking_drop(key, part):
    key = jax.random.fold_in(key, 23)
    return packed_bits(key, (SECTIONS, TOP, TOKENS // 32))


def levels(rng, dims, pieces, low, high):
    def one(dim, blocks):
        draws = jax.random.uniform(jax.random.fold_in(jax.random.fold_in(rng, 6), dim), (blocks,), jnp.float32, low / len(pieces), high / len(pieces))
        return jnp.repeat(jnp.exp(draws), dims[dim] // blocks).reshape((-1,) + (1,) * (len(dims) - dim - 1))

    factor_of = one(*pieces[0])
    for cut in pieces[1:]:
        factor_of = factor_of * one(*cut)
    return factor_of


def deal_out(rng, own, number, rows, amount, top, reach, lean):
    order = jax.random.permutation(rng, amount)
    heavy_load, ordinary = portions_of(amount, rows * top, reach, lean, True), portions_of(amount, rows * top, reach, lean, False)
    places = jnp.arange(amount)

    def named(lengths, rotation):
        used = int((lengths > 0).sum())
        fixed = max(1, used // 4)
        moved = fixed + (places - fixed + rotation * (used - fixed)) % max(1, amount - fixed)
        return jnp.zeros((amount,), jnp.int32).at[order[jnp.where(places < fixed, places, moved)]].set(jnp.asarray(lengths, jnp.int32))

    lengths = jnp.where(number % 4 == 0, named(heavy_load, number // 4), named(ordinary, number - number // 4 - 1))
    mixed = jax.random.permutation(jax.random.fold_in(own, 3), amount)
    source_of, sink = mixed[0:amount // 2 * 2:2], mixed[1:amount // 2 * 2:2]
    margin = jnp.minimum(lengths[source_of] - 1, reach - lengths[sink]) // 2
    margin = jnp.where((source_of == order[0]) | (sink == order[0]) | (lengths[sink] == 0), 0, jnp.maximum(margin, 0))
    moved = jax.random.randint(jax.random.fold_in(own, 4), (amount // 2,), 0, 1 << 20) % (margin + 1)
    lengths = lengths.at[source_of].add(-moved).at[sink].add(moved)
    labels = jnp.searchsorted(jnp.cumsum(lengths), jnp.arange(rows * top), side="right").astype(jnp.int32)
    table = labels.reshape(top, rows).T
    table = table[jax.random.permutation(jax.random.fold_in(own, 1), rows)]
    rotation = jax.random.randint(jax.random.fold_in(own, 2), (rows, 1), 0, top)
    return jnp.take_along_axis(table, (jnp.arange(top)[None, :] + rotation) % top, axis=1)


def portions_of(amount, total, reach, slope, full):
    portions = [(1 << 20) // math.isqrt(rank ** slope) + 1 for rank in range(1, amount + 1)]
    largest = reach if full else min(reach, max(-(-total // amount), total * portions[0] // sum(portions)))
    least = 1 if total - largest >= amount - 1 else 0
    counts, spare = [largest] + [least] * (amount - 1), total - largest - least * (amount - 1)
    while spare > 0:
        candidates = [i for i in range(1, amount) if counts[i] < largest] or [i for i in range(1, amount) if counts[i] < reach]
        pool, remaining = sum([portions[i] for i in candidates]), spare
        for i in candidates:
            extra = min(reach - counts[i], max(1, remaining * portions[i] // pool), spare)
            counts[i] = counts[i] + extra
            spare = spare - extra
    return np.array(counts)


def centred(rng, shape, scale, limit, shards=(), kind=jnp.bfloat16):
    loudness = levels(rng, shape, shards, -0.22, 0.18) if shards else 1.0
    result = jax.random.normal(rng, shape, jnp.float32) * scale * loudness
    return jnp.minimum(jnp.maximum(result, -limit), limit).astype(kind)


def setup_inputs(seed: int = 0) -> dict:
    arg_keys = jax.random.split(jax.random.key(seed), 12)
    rising_in = centred(arg_keys[0], (SECTIONS, TOKENS, D), 1.0, 6.0, ((0, 8), (1, 16)))
    rising_ids_keys = jax.random.split(jax.random.fold_in(arg_keys[1], 1), SECTIONS * TOKENS // TOK_DEV)
    rising_ids_turns = jax.random.permutation(jax.random.fold_in(arg_keys[1], 3), SECTIONS * TOKENS // TOK_DEV)
    rising_ids = jax.vmap(lambda own, number: deal_out(jax.random.fold_in(arg_keys[1], 2), own, number, TOK_DEV, EXPERTS, TOP, CAP, 2))(rising_ids_keys, rising_ids_turns).reshape((SECTIONS, TOKENS, TOP))
    rising_gates = jnp.clip(0.1 + 0.9 * jax.random.uniform(arg_keys[2], (SECTIONS, TOKENS, TOP), jnp.float32) ** levels(arg_keys[2], (SECTIONS, TOKENS, TOP), ((0, 8), (1, 16)), -0.2, 0.2), 0.1, 1.0)
    rising_drop = draw_rising_drop(jax.random.fold_in(arg_keys[11], 71), 0)
    sinking_grad = centred(arg_keys[4], (SECTIONS, TOKENS, D), 1.0, 6.0, ((0, 8), (1, 16)))
    sinking_ids_keys = jax.random.split(jax.random.fold_in(arg_keys[5], 1), SECTIONS * TOKENS // TOK_DEV)
    sinking_ids_turns = jax.random.permutation(jax.random.fold_in(arg_keys[5], 3), SECTIONS * TOKENS // TOK_DEV)
    sinking_ids = jax.vmap(lambda own, number: deal_out(jax.random.fold_in(arg_keys[5], 2), own, number, TOK_DEV, EXPERTS, TOP, CAP, 2))(sinking_ids_keys, sinking_ids_turns).reshape((SECTIONS, TOKENS, TOP))
    sinking_gates = jnp.clip(0.1 + 0.9 * jax.random.uniform(arg_keys[6], (SECTIONS, TOKENS, TOP), jnp.float32) ** levels(arg_keys[6], (SECTIONS, TOKENS, TOP), ((0, 8), (1, 16)), -0.2, 0.2), 0.1, 1.0)
    sinking_drop = draw_sinking_drop(jax.random.fold_in(arg_keys[11], 71), 0)
    sinking_pre = centred(arg_keys[8], (SECTIONS, EXPERTS, SLOTS, HID), 1.0, 6.0, ((0, 8), (1, 8), (3, 2)))
    w_in = centred(arg_keys[9], (SECTIONS, EXPERTS, D, HID), D ** -0.5, 0.0625, ((0, 8), (1, 8), (3, 2)))
    w_out = centred(arg_keys[10], (SECTIONS, EXPERTS, HID, D), HID ** -0.5, 0.1875, ((0, 8), (1, 8), (2, 2)))
    return {"rising_in": rising_in, "rising_ids": rising_ids, "rising_gates": rising_gates, "rising_drop": rising_drop, "sinking_grad": sinking_grad, "sinking_ids": sinking_ids, "sinking_gates": sinking_gates, "sinking_drop": sinking_drop, "sinking_pre": sinking_pre, "w_in": w_in, "w_out": w_out}


keep_scale = 1.0 / 0.9
root_half = 0.7071067811865476
inv_root_tau = 0.3989422804014327


def gelu_value(h):
    return h * (0.5 * (1.0 + lax.erf(h * root_half)))


def gelu_slope(h):
    return 0.5 * (1.0 + lax.erf(h * root_half)) + h * inv_root_tau * jnp.exp(-0.5 * h * h)


def unpack_keep(words):
    shifts = jnp.arange(32, dtype=jnp.int32)
    bits = jnp.right_shift(words[:, :, None], shifts[None, None, :]) & 1
    return bits.reshape(words.shape[0], words.shape[1] * 32).T.astype(jnp.float32)


def slot_of(ids, expert):
    hit = jnp.any(ids == expert, axis=1)
    blocks = hit.reshape(-1, TOK_DEV).astype(jnp.int32)
    place = (jnp.cumsum(blocks, axis=1) - 1).reshape(-1)
    block_id = jnp.arange(TOKENS, dtype=jnp.int32) // TOK_DEV
    slot = jnp.where(hit, block_id * CAP + place, SLOTS)
    return slot.astype(jnp.int32)


def token_rows(values, slot):
    table = jnp.zeros((SLOTS + 1, values.shape[1]), values.dtype).at[slot].set(values)
    return table[:SLOTS]


def read_back(values, slot):
    padded = jnp.concatenate([values, jnp.zeros((1, values.shape[1]), values.dtype)], axis=0)
    return padded[slot].astype(jnp.float32)


def rising_section(inputs, ids, gates, words, w_in, w_out):
    coef = (unpack_keep(words) * gates) * keep_scale
    half = HID // N_DP
    total = jnp.zeros((TOKENS, D), jnp.float32)
    for expert in range(EXPERTS):
        slot = slot_of(ids, expert)
        rows = token_rows(inputs, slot)
        pre = jnp.dot(rows, w_in[expert], preferred_element_type=jnp.float32)
        act = gelu_value(pre).astype(jnp.bfloat16)
        summed = jnp.zeros((SLOTS, D), jnp.float32)
        for block in range(N_DP):
            piece = jnp.dot(act[:, block * half:(block + 1) * half], w_out[expert, block * half:(block + 1) * half], preferred_element_type=jnp.float32)
            summed = summed + piece.astype(jnp.bfloat16).astype(jnp.float32)
        expert_out = summed.astype(jnp.bfloat16)
        weight = jnp.sum(jnp.where(ids == expert, coef, 0.0), axis=1)
        total = total + weight[:, None] * read_back(expert_out, slot)
    return total.astype(jnp.bfloat16)


def sinking_section(grad, ids, gates, words, saved, w_in, w_out):
    coef = (unpack_keep(words) * gates) * keep_scale
    half = HID // N_DP
    grad_f = grad.astype(jnp.float32)
    total = jnp.zeros((TOKENS, D), jnp.float32)
    for expert in range(EXPERTS):
        slot = slot_of(ids, expert)
        weight = jnp.sum(jnp.where(ids == expert, coef, 0.0), axis=1)
        rows = token_rows((weight[:, None] * grad_f).astype(jnp.bfloat16), slot)
        summed = jnp.zeros((SLOTS, D), jnp.float32)
        for block in range(N_DP):
            cols = slice(block * half, (block + 1) * half)
            back_act = jnp.dot(rows, w_out[expert, cols].T, preferred_element_type=jnp.float32)
            back_pre = (back_act * gelu_slope(saved[expert][:, cols].astype(jnp.float32))).astype(jnp.bfloat16)
            piece = jnp.dot(back_pre, w_in[expert][:, cols].T, preferred_element_type=jnp.float32)
            summed = summed + piece.astype(jnp.bfloat16).astype(jnp.float32)
        expert_grad = summed.astype(jnp.bfloat16)
        total = total + read_back(expert_grad, slot)
    return total.astype(jnp.bfloat16)


def reference(rising_in, rising_ids, rising_gates, rising_drop, sinking_grad, sinking_ids, sinking_gates, sinking_drop, sinking_pre, w_in, w_out):
    zero = jnp.zeros((TOKENS, D), jnp.bfloat16)
    ahead = [zero]
    behind = [zero]
    for section in range(SECTIONS - 1):
        ahead.append(rising_section(rising_in[section], rising_ids[section], rising_gates[section], rising_drop[section], w_in[section], w_out[section]))
        behind.append(sinking_section(sinking_grad[section], sinking_ids[section], sinking_gates[section], sinking_drop[section], sinking_pre[section], w_in[section], w_out[section]))
    return jnp.stack(ahead), jnp.stack(behind)
```

```python
import jax
import jax.numpy as jnp
from jax import lax
from jax.sharding import PartitionSpec as P

keep_scale = 1.0 / 0.9
root_half = 0.7071067811865476
inv_root_tau = 0.3989422804014327


def from_behind(block, axis, distance):
    devices = range(lax.axis_size(axis))
    route = [(i - distance, i) for i in devices if i - distance in devices]
    return lax.ppermute(block, axis, route)


def swap_cores(block):
    return lax.ppermute(block, "dp", [(0, 1), (1, 0)])


def gelu_value(h):
    return h * (0.5 * (1.0 + lax.erf(h * root_half)))


def gelu_slope(h):
    return 0.5 * (1.0 + lax.erf(h * root_half)) + h * inv_root_tau * jnp.exp(-0.5 * h * h)


def unpack_keep(words):
    shifts = jnp.arange(32, dtype=jnp.int32)
    bits = jnp.right_shift(words[:, :, None], shifts[None, None, :]) & 1
    return bits.reshape(words.shape[0], words.shape[1] * 32).T.astype(jnp.float32)


def routing(ids, owners, cap):
    count = ids.shape[0]
    names = jnp.arange(owners, dtype=jnp.int32)
    named = ids[:, :, None] == names[None, None, :]
    hit = jnp.any(named, axis=1).astype(jnp.int32)
    place = jnp.cumsum(hit, axis=0) - 1
    seat = jnp.sum(jnp.where(named, place[:, None, :], 0), axis=2)
    return ids * cap + seat


def pick(slots, rows):
    seats = jnp.arange(rows, dtype=jnp.int32)
    return [(slots[:, k : k + 1] == seats[None, :]) for k in range(slots.shape[1])]


def spread(hot, values):
    return lax.dot_general(
        hot.astype(jnp.bfloat16), values, (((0,), (0,)), ((), ())), preferred_element_type=jnp.float32
    )


def dispatch(send):
    own = lax.all_to_all(send, "expert", split_axis=0, concat_axis=0, tiled=True)
    own = own.reshape(-1, own.shape[2])
    return own, swap_cores(own)


def combine(own, other, owners):
    added = own.astype(jnp.float32) + swap_cores(other).astype(jnp.float32)
    added = added.astype(jnp.bfloat16).reshape(owners, -1, own.shape[1])
    back = lax.all_to_all(added, "expert", split_axis=0, concat_axis=0, tiled=True)
    return back.reshape(-1, own.shape[1])


def local(
    rising_in,
    rising_ids,
    rising_gates,
    rising_drop,
    sinking_grad,
    sinking_ids,
    sinking_gates,
    sinking_drop,
    sinking_pre,
    w_in,
    w_out,
):
    owners = lax.axis_size("expert")
    pairs = lax.axis_size("dp")
    me = lax.axis_index("dp")
    slots = sinking_pre.shape[2]
    cap = slots // (owners * pairs)
    rows = owners * cap
    wi, wo = w_in[0, 0], w_out[0, 0]
    coef_one = unpack_keep(rising_drop[0]) * rising_gates[0] * keep_scale
    coef_two = unpack_keep(sinking_drop[0]) * sinking_gates[0] * keep_scale
    hot_one = pick(routing(rising_ids[0], owners, cap), rows)
    hot_two = pick(routing(sinking_ids[0], owners, cap), rows)

    send_one = spread(hot_one[0] | hot_one[1], rising_in[0]).astype(jnp.bfloat16)
    weight = jnp.sum(
        sum(jnp.where(hot_two[k], coef_two[:, k : k + 1], 0.0) for k in range(2)), axis=0
    )
    send_two = (weight[:, None] * spread(hot_two[0] | hot_two[1], sinking_grad[0])).astype(jnp.bfloat16)

    got_one = dispatch(send_one.reshape(owners, cap, -1))
    got_two = dispatch(send_two.reshape(owners, cap, -1))

    def forward_part(got):
        act = gelu_value(jnp.dot(got, wi, preferred_element_type=jnp.float32)).astype(jnp.bfloat16)
        return jnp.dot(act, wo, preferred_element_type=jnp.float32).astype(jnp.bfloat16)

    pre = sinking_pre[0, 0].reshape(owners, pairs, cap, -1)

    def backward_part(got, core):
        saved = lax.dynamic_index_in_dim(pre, core, 1, keepdims=False).reshape(rows, -1)
        act = lax.dot_general(got, wo, (((1,), (1,)), ((), ())), preferred_element_type=jnp.float32)
        mid = (act * gelu_slope(saved.astype(jnp.float32))).astype(jnp.bfloat16)
        return lax.dot_general(
            mid, wi, (((1,), (1,)), ((), ())), preferred_element_type=jnp.float32
        ).astype(jnp.bfloat16)

    back_one = combine(forward_part(got_one[0]), forward_part(got_one[1]), owners)
    back_two = combine(backward_part(got_two[0], me), backward_part(got_two[1], 1 - me), owners)

    def collect(hot, back):
        return jnp.dot(hot.astype(jnp.bfloat16), back, preferred_element_type=jnp.float32)

    forward = sum(coef_one[:, k : k + 1] * collect(hot_one[k], back_one) for k in range(2))
    handed_forward = from_behind(forward.astype(jnp.bfloat16)[None], "pipe", 1)
    backward = collect(hot_two[0] | hot_two[1], back_two)
    handed_backward = from_behind(backward.astype(jnp.bfloat16)[None], "pipe", 1)
    return (handed_forward, handed_backward)


def solution(mesh):
    placed = (
        P("pipe", ("expert", "dp"), None),
        P("pipe", ("expert", "dp"), None),
        P("pipe", ("expert", "dp"), None),
        P("pipe", None, ("expert", "dp")),
        P("pipe", ("expert", "dp"), None),
        P("pipe", ("expert", "dp"), None),
        P("pipe", ("expert", "dp"), None),
        P("pipe", None, ("expert", "dp")),
        P("pipe", "expert", None, "dp"),
        P("pipe", "expert", None, "dp"),
        P("pipe", "expert", "dp", None),
    )
    return jax.shard_map(
        local,
        mesh=mesh,
        in_specs=placed,
        out_specs=(P("pipe", ("expert", "dp"), None), P("pipe", ("expert", "dp"), None)),
        check_vma=False,
    )
```

```python
import functools

import jax
import jax.experimental.pallas as pl
import jax.experimental.pallas.tpu as pltpu
import jax.numpy as jnp
from jax import lax
from jax.sharding import PartitionSpec as P

keep_scale = 1.0 / 0.9
root_half = 0.7071067811865476
inv_root_tau = 0.3989422804014327
MESH = pl.DeviceIdType.MESH
CHUNK = 1024


def gelu_value(h):
    return h * (0.5 * (1.0 + lax.erf(h * root_half)))


def gelu_slope(h):
    return 0.5 * (1.0 + lax.erf(h * root_half)) + h * inv_root_tau * jnp.exp(-0.5 * h * h)


def unpack_keep(words):
    shifts = jnp.arange(32, dtype=jnp.int32)
    bits = jnp.right_shift(words[:, :, None], shifts[None, None, :]) & 1
    return bits.reshape(words.shape[0], words.shape[1] * 32).T.astype(jnp.float32)


def routing(ids, owners, cap):
    names = jnp.arange(owners, dtype=jnp.int32)
    named = ids[:, :, None] == names[None, None, :]
    hit = jnp.any(named, axis=1).astype(jnp.int32)
    place = jnp.cumsum(hit, axis=0) - 1
    seat = jnp.sum(jnp.where(named, place[:, None, :], 0), axis=2)
    return ids * cap + seat


def relay(
    sizes,
    send_one, send_two, meta, saved, w_in, w_out,
    out_one, out_two, back_one, back_two,
    wi, wo, got_one, got_two, other_one, other_two, acc, act, pre, metas, zeros, staged, held,
    load_sem, meta_sem, d_send, d_recv, s_send, s_recv, x_send, x_recv, c_send, c_recv,
    r_sem, o_send, o_recv,
):
    owners, cap, steps, width, sections = sizes
    rows = owners * cap
    p, me, core = lax.axis_index("pipe"), lax.axis_index("expert"), lax.axis_index("dp")
    odd = lax.rem(p, 2)
    across = p + 1 - 2 * odd
    sends_on = jnp.logical_and(odd == 0, p + 2 < sections)
    gets_on = jnp.logical_and(odd == 0, p >= 2)

    barrier = pltpu.get_barrier_semaphore()
    for d in range(1, owners):
        pl.semaphore_signal(
            barrier, device_id=(p, lax.rem(me + d, owners), core), device_id_type=MESH
        )
    for d in range(owners):
        pl.semaphore_signal(
            barrier, device_id=(across, lax.rem(me + d, owners), core), device_id_type=MESH
        )
    pl.semaphore_signal(barrier, device_id=(p, me, 1 - core), device_id_type=MESH)

    @pl.when(gets_on)
    def _():
        pl.semaphore_signal(barrier, device_id=(p - 2, me, core), device_id_type=MESH)

    load_in = pltpu.make_async_copy(w_in, wi, load_sem.at[0])
    load_out = pltpu.make_async_copy(w_out, wo, load_sem.at[1])
    load_pre = [
        pltpu.make_async_copy(saved.at[:, core if side == 0 else 1 - core], pre.at[side], load_sem.at[2 + side])
        for side in range(2)
    ]
    load_in.start()
    load_out.start()
    for copy in load_pre:
        copy.start()
    zeros[...] = jnp.zeros_like(zeros)

    pl.semaphore_wait(barrier, 2 * owners + jnp.where(sends_on, 1, 0))

    sends, gots, others = (send_one, send_two), (got_one, got_two), (other_one, other_two)
    backs, outs = (back_one, back_two), (out_one, out_two)

    def columns(j):
        return pl.ds(pl.multiple_of(j * width, width), width)

    def dispatch(m, j):
        for d in range(1, owners):
            to = lax.rem(me + d, owners)
            pltpu.make_async_remote_copy(
                sends[m].at[to, :, columns(j)], gots[m].at[j, 0, me],
                d_send.at[m, j], d_recv.at[m, j],
                device_id=(p, to, core), device_id_type=MESH,
            ).start()
        pltpu.make_async_copy(
            sends[m].at[me, :, columns(j)], gots[m].at[j, 0, me], d_recv.at[m, j]
        ).start()

    def swap(m, j):
        return pltpu.make_async_remote_copy(
            gots[m].at[j, 0], gots[m].at[j, 1], s_send.at[m, j], s_recv.at[m, j],
            device_id=(p, me, 1 - core), device_id_type=MESH,
        )

    def cross(m, j):
        return pltpu.make_async_remote_copy(
            gots[m].at[j, 1], others[m].at[j], x_send.at[m, j], x_recv.at[m, j],
            device_id=(p, me, 1 - core), device_id_type=MESH,
        )

    def whole(ref, sem):
        return pltpu.make_async_copy(ref, ref, sem)

    def flat(ref):
        return ref[...].reshape(rows, width)

    def receive(m, j):
        whole(gots[m].at[j, 0], d_recv.at[m, j]).wait()
        swap(m, j).start()
        for side in range(2):
            if side == 1:
                swap(m, j).wait()
            block = flat(gots[m].at[j, side])
            if m == 0:
                acc[m, side] += jnp.dot(
                    block, wi[columns(j), :], preferred_element_type=jnp.float32
                )
            else:
                acc[m, side] += lax.dot_general(
                    block, wo[:, columns(j)], (((1,), (1,)), ((), ())),
                    preferred_element_type=jnp.float32,
                )

    def project(m, j, side):
        if m == 0:
            part = jnp.dot(act[m, side], wo[:, columns(j)], preferred_element_type=jnp.float32)
        else:
            part = lax.dot_general(
                act[m, side], wi[columns(j), :], (((1,), (1,)), ((), ())),
                preferred_element_type=jnp.float32,
            )
        return part.reshape(owners, cap, width).astype(jnp.bfloat16)

    def give_back(m, j):
        gots[m][j, 1] = project(m, j, 1)
        cross(m, j).start()
        part = project(m, j, 0)
        cross(m, j).wait()
        gots[m][j, 0] = (
            part.astype(jnp.float32) + others[m][j].astype(jnp.float32)
        ).astype(jnp.bfloat16)
        for d in range(owners):
            to = lax.rem(me + d, owners)
            pltpu.make_async_remote_copy(
                gots[m].at[j, 0, to], backs[m].at[j, me], c_send.at[m, j], c_recv.at[m, j],
                device_id=(across, to, core), device_id_type=MESH,
            ).start()

    def out_local(m, j):
        return pltpu.make_async_copy(staged.at[m, j], outs[m].at[:, columns(j)], o_send.at[m, j])

    def out_zero(m, j):
        return pltpu.make_async_copy(zeros, outs[m].at[:, columns(j)], o_recv.at[m, j])

    def out_on(m, j):
        return pltpu.make_async_remote_copy(
            staged.at[m, j], outs[m].at[:, columns(j)], o_send.at[m, j], o_recv.at[m, j],
            device_id=(lax.rem(p + 2, sections), me, core), device_id_type=MESH,
        )

    def collect(m, j):
        whole(backs[m].at[j], c_recv.at[m, j]).wait()
        fetch = pltpu.make_async_copy(backs[m].at[j], held, r_sem)
        fetch.start()
        seats = lax.broadcasted_iota(jnp.int32, (metas.shape[1], rows), 1).astype(jnp.float32)
        base = 4 * m
        hot = [(metas[1, :, base + k : base + k + 1] == seats) for k in range(2)]
        fetch.wait()
        block = flat(held)

        def rows_of(mask):
            return jnp.dot(
                jnp.where(mask, 1.0, 0.0).astype(jnp.bfloat16), block,
                preferred_element_type=jnp.float32,
            )

        if m == 0:
            total = (
                metas[1, :, base + 2 : base + 3] * rows_of(hot[0])
                + metas[1, :, base + 3 : base + 4] * rows_of(hot[1])
            )
        else:
            total = rows_of(jnp.logical_or(hot[0], hot[1]))
        staged[m, j] = total.astype(jnp.bfloat16)

        @pl.when(odd == 1)
        def _():
            out_local(m, j).start()

        @pl.when(sends_on)
        def _():
            out_on(m, j).start()

        @pl.when(p == 0)
        def _():
            out_zero(m, j).start()

    def loop(body):
        lax.fori_loop(0, steps, lambda j, _: (body(j), 0)[1], 0)

    meta_local = pltpu.make_async_copy(meta, metas.at[0], meta_sem.at[2])
    meta_far = pltpu.make_async_remote_copy(
        meta, metas.at[1], meta_sem.at[0], meta_sem.at[1],
        device_id=(across, me, core), device_id_type=MESH,
    )
    meta_local.start()
    loop(lambda j: dispatch(0, j))
    meta_far.start()
    acc[...] = jnp.zeros_like(acc)
    load_in.wait()

    def first(j):
        dispatch(1, j)
        receive(0, j)

    loop(first)
    for side in range(2):
        act[0, side] = gelu_value(acc[0, side]).astype(jnp.bfloat16)
    load_out.wait()

    def second(j):
        give_back(0, j)
        receive(1, j)

    loop(second)
    for copy in load_pre:
        copy.wait()
    for side in range(2):
        slope = gelu_slope(pre[side].astype(jnp.float32)).reshape(rows, pre.shape[3])
        act[1, side] = (acc[1, side] * slope).astype(jnp.bfloat16)
    meta_local.wait()
    meta_far.wait()

    def third(j):
        give_back(1, j)
        collect(0, j)

    loop(third)
    loop(lambda j: collect(1, j))

    def drain(j):
        for m in range(2):
            part = gots[m].at[j, 0]
            whole(part.at[pl.ds(0, owners - 1)], d_send.at[m, j]).wait()
            whole(part, c_send.at[m, j]).wait()

            @pl.when(odd == 1)
            def _():
                out_local(m, j).wait()

            @pl.when(sends_on)
            def _():
                out_on(m, j).wait_send()

            @pl.when(gets_on)
            def _():
                out_on(m, j).wait_recv()

            @pl.when(p == 0)
            def _():
                out_zero(m, j).wait()

    loop(drain)


def local(
    rising_in,
    rising_ids,
    rising_gates,
    rising_drop,
    sinking_grad,
    sinking_ids,
    sinking_gates,
    sinking_drop,
    sinking_pre,
    w_in,
    w_out,
):
    owners, pairs, sections = lax.axis_size("expert"), lax.axis_size("dp"), lax.axis_size("pipe")
    slots, half = sinking_pre.shape[2:]
    count, model = rising_in.shape[1:]
    cap = slots // (owners * pairs)
    rows = owners * cap
    width = CHUNK
    steps = model // width
    coef_one = unpack_keep(rising_drop[0]) * rising_gates[0] * keep_scale
    coef_two = unpack_keep(sinking_drop[0]) * sinking_gates[0] * keep_scale
    seats_one = routing(rising_ids[0], owners, cap)
    seats_two = routing(sinking_ids[0], owners, cap)
    meta = jnp.concatenate(
        [
            seats_one.astype(jnp.float32), coef_one, seats_two.astype(jnp.float32), coef_two,
            jnp.zeros((count, 120), jnp.float32),
        ],
        axis=1,
    )

    def hot(seats, k):
        return seats[:, k : k + 1] == jnp.arange(rows, dtype=jnp.int32)[None, :]

    def spread(mask, values):
        return lax.dot_general(
            mask.astype(jnp.bfloat16), values, (((0,), (0,)), ((), ())),
            preferred_element_type=jnp.float32,
        )

    send_one = spread(hot(seats_one, 0) | hot(seats_one, 1), rising_in[0]).astype(jnp.bfloat16)
    weight = jnp.sum(
        sum(jnp.where(hot(seats_two, k), coef_two[:, k : k + 1], 0.0) for k in range(2)), axis=0
    )
    send_two = (
        weight[:, None] * spread(hot(seats_two, 0) | hot(seats_two, 1), sinking_grad[0])
    ).astype(jnp.bfloat16)

    hbm = pl.BlockSpec(memory_space=pl.ANY)
    b16, f32 = jnp.bfloat16, jnp.float32
    dma = pltpu.SemaphoreType.DMA
    result = pl.pallas_call(
        functools.partial(relay, (owners, cap, steps, width, sections)),
        out_shape=(
            jax.ShapeDtypeStruct((count, model), b16),
            jax.ShapeDtypeStruct((count, model), b16),
            jax.ShapeDtypeStruct((steps, owners, cap, width), b16),
            jax.ShapeDtypeStruct((steps, owners, cap, width), b16),
        ),
        in_specs=[hbm] * 6,
        out_specs=(hbm,) * 4,
        scratch_shapes=[
            pltpu.VMEM((model, half), b16),
            pltpu.VMEM((half, model), b16),
            pltpu.VMEM((steps, 2, owners, cap, width), b16),
            pltpu.VMEM((steps, 2, owners, cap, width), b16),
            pltpu.VMEM((steps, owners, cap, width), b16),
            pltpu.VMEM((steps, owners, cap, width), b16),
            pltpu.VMEM((2, 2, rows, half), f32),
            pltpu.VMEM((2, 2, rows, half), b16),
            pltpu.VMEM((2, owners, cap, half), b16),
            pltpu.VMEM((2, count, 128), f32),
            pltpu.VMEM((count, width), b16),
            pltpu.VMEM((2, steps, count, width), b16),
            pltpu.VMEM((owners, cap, width), b16),
            dma((4,)),
            dma((3,)),
        ]
        + [dma((2, steps))] * 8
        + [dma, dma((2, steps)), dma((2, steps))],
        compiler_params=pltpu.CompilerParams(
            collective_id=0, has_side_effects=True, vmem_limit_bytes=62 << 20
        ),
        cost_estimate=pl.CostEstimate(
            flops=16 * rows * model * half, bytes_accessed=60_000_000, transcendentals=4 * rows * half
        ),
    )(
        send_one.reshape(owners, cap, model),
        send_two.reshape(owners, cap, model),
        meta,
        sinking_pre.reshape(owners, pairs, cap, half),
        w_in[0, 0],
        w_out[0, 0],
    )
    return (result[0][None], result[1][None])


def solution(mesh):
    placed = (
        P("pipe", ("expert", "dp"), None),
        P("pipe", ("expert", "dp"), None),
        P("pipe", ("expert", "dp"), None),
        P("pipe", None, ("expert", "dp")),
        P("pipe", ("expert", "dp"), None),
        P("pipe", ("expert", "dp"), None),
        P("pipe", ("expert", "dp"), None),
        P("pipe", None, ("expert", "dp")),
        P("pipe", "expert", None, "dp"),
        P("pipe", "expert", None, "dp"),
        P("pipe", "expert", "dp", None),
    )
    return jax.shard_map(
        local,
        mesh=mesh,
        in_specs=placed,
        out_specs=(P("pipe", ("expert", "dp"), None), P("pipe", ("expert", "dp"), None)),
        check_vma=False,
    )
```

```python
import functools

import jax
import jax.experimental.pallas as pl
import jax.experimental.pallas.tpu as pltpu
import jax.numpy as jnp
from jax import lax
from jax.sharding import PartitionSpec as P

keep_scale = 1.0 / 0.9
root_half = 0.7071067811865476
inv_root_tau = 0.3989422804014327
MESH = pl.DeviceIdType.MESH
CHUNK = 512


def gelu_value(h):
    return h * (0.5 * (1.0 + lax.erf(h * root_half)))


def gelu_slope(h):
    return 0.5 * (1.0 + lax.erf(h * root_half)) + h * inv_root_tau * jnp.exp(-0.5 * h * h)


def coefficients(words, gates):
    lanes = lax.broadcasted_iota(jnp.int32, gates.shape, 1)
    word = jnp.zeros(gates.shape, jnp.int32)
    for q in range(words.shape[1]):
        word = jnp.where(lanes // 32 == q, words[:, q : q + 1], word)
    keep = (jnp.right_shift(word, lanes % 32) & 1).astype(jnp.float32)
    return keep * gates * keep_scale


def routing(ids, owners, cap):
    top, count = ids.shape
    names = lax.broadcasted_iota(jnp.int32, (owners, count), 0)
    named = [ids[k : k + 1, :] == names for k in range(top)]
    hit = jnp.where(jnp.logical_or(named[0], named[1]), 1.0, 0.0)
    upto = lax.broadcasted_iota(jnp.int32, (count, count), 0) <= lax.broadcasted_iota(
        jnp.int32, (count, count), 1
    )
    place = jnp.dot(hit, jnp.where(upto, 1.0, 0.0), preferred_element_type=jnp.float32)
    row = place - 1.0 + (names * cap).astype(jnp.float32)
    return [jnp.sum(jnp.where(n, row, 0.0), axis=0, keepdims=True) for n in named]


def upright(row):
    n = row.shape[1]
    same = lax.broadcasted_iota(jnp.int32, (n, n), 0) == lax.broadcasted_iota(jnp.int32, (n, n), 1)
    return jnp.sum(jnp.where(same, row, 0.0), axis=1, keepdims=True)


def relay(
    sizes,
    ids_one, gates_one, drop_one, ids_two, gates_two, drop_two,
    rows_one, rows_two, saved, w_in, w_out,
    out_one, out_two,
    wi, wo, got_one, got_two, other_one, other_two, back_one, back_two,
    acc, act, pre, metas, zeros, staged, put, scale, hot, coef,
    load_sem, meta_sem, d_send, d_recv, s_send, s_recv, x_send, x_recv, c_send, c_recv,
    o_send, o_recv, l_sem,
):
    owners, cap, steps, width, sections = sizes
    rows = owners * cap
    p, me, core = lax.axis_index("pipe"), lax.axis_index("expert"), lax.axis_index("dp")
    odd = lax.rem(p, 2)
    across = p + 1 - 2 * odd
    sends_on = jnp.logical_and(odd == 0, p + 2 < sections)
    gets_on = jnp.logical_and(odd == 0, p >= 2)

    barrier = pltpu.get_barrier_semaphore()
    for d in range(1, owners):
        pl.semaphore_signal(
            barrier, device_id=(p, lax.rem(me + d, owners), core), device_id_type=MESH
        )
    for d in range(owners):
        pl.semaphore_signal(
            barrier, device_id=(across, lax.rem(me + d, owners), core), device_id_type=MESH
        )
    pl.semaphore_signal(barrier, device_id=(p, me, 1 - core), device_id_type=MESH)

    @pl.when(gets_on)
    def _():
        pl.semaphore_signal(barrier, device_id=(p - 2, me, core), device_id_type=MESH)

    load_in = pltpu.make_async_copy(w_in, wi, load_sem.at[0])
    load_out = pltpu.make_async_copy(w_out, wo, load_sem.at[1])
    load_pre = [
        pltpu.make_async_copy(saved.at[:, core if side == 0 else 1 - core], pre.at[side], load_sem.at[2 + side])
        for side in range(2)
    ]
    tokens = (rows_one, rows_two)

    def columns(j):
        return pl.ds(pl.multiple_of(j * width, width), width)

    def load_rows(m, j):
        return pltpu.make_async_copy(tokens[m].at[:, columns(j)], staged.at[m, j], l_sem.at[m, j])

    def loop(body):
        lax.fori_loop(0, steps, lambda j, _: (body(j), 0)[1], 0)

    loop(lambda j: load_rows(0, j).start())
    load_in.start()
    loop(lambda j: load_rows(1, j).start())
    load_out.start()
    for copy in load_pre:
        copy.start()

    count = metas.shape[2]
    places = lax.broadcasted_iota(jnp.int32, (rows, count), 0).astype(jnp.float32)
    for m, (ids, gates, words) in enumerate(
        ((ids_one, gates_one, drop_one), (ids_two, gates_two, drop_two))
    ):
        seats = routing(ids[...], owners, cap)
        weights = coefficients(words[...], gates[...])
        mine = [places == seat for seat in seats]
        put[m] = jnp.where(jnp.logical_or(mine[0], mine[1]), 1.0, 0.0).astype(jnp.bfloat16)
        for k in range(2):
            metas[0, 4 * m + k : 4 * m + k + 1, :] = seats[k]
        metas[0, 4 * m + 2 : 4 * m + 4, :] = weights
        if m == 1:
            scale[...] = jnp.sum(
                jnp.where(mine[0], weights[0:1], 0.0) + jnp.where(mine[1], weights[1:2], 0.0),
                axis=1, keepdims=True,
            )
    zeros[...] = jnp.zeros_like(zeros)

    pl.semaphore_wait(barrier, 2 * owners + jnp.where(sends_on, 1, 0))

    gots, others = (got_one, got_two), (other_one, other_two)
    backs, outs = (back_one, back_two), (out_one, out_two)

    def dispatch(m, j):
        load_rows(m, j).wait()
        picked = jnp.dot(put[m], staged[m, j], preferred_element_type=jnp.float32)
        if m == 1:
            picked = scale[...] * picked
        others[m][j] = picked.reshape(owners, cap, width).astype(jnp.bfloat16)
        for d in range(1, owners):
            to = lax.rem(me + d, owners)
            pltpu.make_async_remote_copy(
                others[m].at[j, to], gots[m].at[j, 0, me],
                d_send.at[m, j], d_recv.at[m, j],
                device_id=(p, to, core), device_id_type=MESH,
            ).start()
        pltpu.make_async_copy(
            others[m].at[j, me], gots[m].at[j, 0, me], d_recv.at[m, j]
        ).start()

    def swap(m, j):
        return pltpu.make_async_remote_copy(
            gots[m].at[j, 0], gots[m].at[j, 1], s_send.at[m, j], s_recv.at[m, j],
            device_id=(p, me, 1 - core), device_id_type=MESH,
        )

    def cross(m, j):
        return pltpu.make_async_remote_copy(
            gots[m].at[j, 1], others[m].at[j], x_send.at[m, j], x_recv.at[m, j],
            device_id=(p, me, 1 - core), device_id_type=MESH,
        )

    def whole(ref, sem):
        return pltpu.make_async_copy(ref, ref, sem)

    def flat(ref):
        return ref[...].reshape(rows, width)

    def receive(m, j):
        whole(others[m].at[j, pl.ds(0, owners - 1)], d_send.at[m, j]).wait()
        whole(gots[m].at[j, 0], d_recv.at[m, j]).wait()
        swap(m, j).start()
        for side in range(2):
            if side == 1:
                swap(m, j).wait()
            block = flat(gots[m].at[j, side])
            if m == 0:
                acc[m, side] += jnp.dot(
                    block, wi[columns(j), :], preferred_element_type=jnp.float32
                )
            else:
                acc[m, side] += lax.dot_general(
                    block, wo[:, columns(j)], (((1,), (1,)), ((), ())),
                    preferred_element_type=jnp.float32,
                )

    def project(m, j, side):
        if m == 0:
            part = jnp.dot(act[m, side], wo[:, columns(j)], preferred_element_type=jnp.float32)
        else:
            part = lax.dot_general(
                act[m, side], wi[columns(j), :], (((1,), (1,)), ((), ())),
                preferred_element_type=jnp.float32,
            )
        return part.reshape(owners, cap, width).astype(jnp.bfloat16)

    def give_back(m, j):
        gots[m][j, 1] = project(m, j, 1)
        cross(m, j).start()
        part = project(m, j, 0)
        cross(m, j).wait()
        gots[m][j, 0] = (
            part.astype(jnp.float32) + others[m][j].astype(jnp.float32)
        ).astype(jnp.bfloat16)
        for d in range(owners):
            to = lax.rem(me + d, owners)
            pltpu.make_async_remote_copy(
                gots[m].at[j, 0, to], backs[m].at[j, me], c_send.at[m, j], c_recv.at[m, j],
                device_id=(across, to, core), device_id_type=MESH,
            ).start()

    def out_local(m, j):
        return pltpu.make_async_copy(staged.at[m, j], outs[m].at[:, columns(j)], o_send.at[m, j])

    def out_zero(m, j):
        return pltpu.make_async_copy(zeros, outs[m].at[:, columns(j)], o_recv.at[m, j])

    def out_on(m, j):
        return pltpu.make_async_remote_copy(
            staged.at[m, j], outs[m].at[:, columns(j)], o_send.at[m, j], o_recv.at[m, j],
            device_id=(lax.rem(p + 2, sections), me, core), device_id_type=MESH,
        )

    def collect(m, j):
        whole(backs[m].at[j], c_recv.at[m, j]).wait()
        block = flat(backs[m].at[j])

        def rows_of(n):
            return jnp.dot(hot[n], block, preferred_element_type=jnp.float32)

        if m == 0:
            total = coef[0] * rows_of(0) + coef[1] * rows_of(1)
        else:
            total = rows_of(2)
        staged[m, j] = total.astype(jnp.bfloat16)

        @pl.when(odd == 1)
        def _():
            out_local(m, j).start()

        @pl.when(sends_on)
        def _():
            out_on(m, j).start()

        @pl.when(p == 0)
        def _():
            out_zero(m, j).start()

    meta_far = pltpu.make_async_remote_copy(
        metas.at[0], metas.at[1], meta_sem.at[0], meta_sem.at[1],
        device_id=(across, me, core), device_id_type=MESH,
    )
    loop(lambda j: dispatch(0, j))
    meta_far.start()
    acc[...] = jnp.zeros_like(acc)
    load_in.wait()

    def first(j):
        dispatch(1, j)
        receive(0, j)

    loop(first)
    for side in range(2):
        act[0, side] = gelu_value(acc[0, side]).astype(jnp.bfloat16)
    load_out.wait()

    def second(j):
        give_back(0, j)
        receive(1, j)

    loop(second)
    for copy in load_pre:
        copy.wait()
    for side in range(2):
        slope = gelu_slope(pre[side].astype(jnp.float32)).reshape(rows, pre.shape[3])
        act[1, side] = (acc[1, side] * slope).astype(jnp.bfloat16)
    meta_far.wait()
    seat_at = lax.broadcasted_iota(jnp.int32, (count, rows), 1).astype(jnp.float32)

    def theirs(n):
        return seat_at == upright(metas[1, n : n + 1, :])

    for k in range(2):
        hot[k] = jnp.where(theirs(k), 1.0, 0.0).astype(jnp.bfloat16)
        coef[k] = upright(metas[1, 2 + k : 3 + k, :])
    hot[2] = jnp.where(jnp.logical_or(theirs(4), theirs(5)), 1.0, 0.0).astype(jnp.bfloat16)

    def third(j):
        give_back(1, j)
        collect(0, j)

    loop(third)
    loop(lambda j: collect(1, j))

    def drain(j):
        for m in range(2):
            part = gots[m].at[j, 0]
            whole(part, c_send.at[m, j]).wait()

            @pl.when(odd == 1)
            def _():
                out_local(m, j).wait()

            @pl.when(sends_on)
            def _():
                out_on(m, j).wait_send()

            @pl.when(gets_on)
            def _():
                out_on(m, j).wait_recv()

            @pl.when(p == 0)
            def _():
                out_zero(m, j).wait()

    loop(drain)


def local(
    rising_in,
    rising_ids,
    rising_gates,
    rising_drop,
    sinking_grad,
    sinking_ids,
    sinking_gates,
    sinking_drop,
    sinking_pre,
    w_in,
    w_out,
):
    owners, pairs, sections = lax.axis_size("expert"), lax.axis_size("dp"), lax.axis_size("pipe")
    slots, half = sinking_pre.shape[2:]
    count, model = rising_in.shape[1:]
    cap = slots // (owners * pairs)
    rows = owners * cap
    width = CHUNK
    steps = model // width
    hbm = pl.BlockSpec(memory_space=pl.ANY)
    b16, f32 = jnp.bfloat16, jnp.float32
    dma = pltpu.SemaphoreType.DMA
    result = pl.pallas_call(
        functools.partial(relay, (owners, cap, steps, width, sections)),
        out_shape=(
            jax.ShapeDtypeStruct((count, model), b16),
            jax.ShapeDtypeStruct((count, model), b16),
        ),
        in_specs=[pl.BlockSpec(memory_space=pltpu.VMEM)] * 6 + [hbm] * 5,
        out_specs=(hbm,) * 2,
        scratch_shapes=[
            pltpu.VMEM((model, half), b16),
            pltpu.VMEM((half, model), b16),
            pltpu.VMEM((steps, 2, owners, cap, width), b16),
            pltpu.VMEM((steps, 2, owners, cap, width), b16),
            pltpu.VMEM((steps, owners, cap, width), b16),
            pltpu.VMEM((steps, owners, cap, width), b16),
            pltpu.VMEM((steps, owners, cap, width), b16),
            pltpu.VMEM((steps, owners, cap, width), b16),
            pltpu.VMEM((2, 2, rows, half), f32),
            pltpu.VMEM((2, 2, rows, half), b16),
            pltpu.VMEM((2, owners, cap, half), b16),
            pltpu.VMEM((2, 8, count), f32),
            pltpu.VMEM((count, width), b16),
            pltpu.VMEM((2, steps, count, width), b16),
            pltpu.VMEM((2, rows, count), b16),
            pltpu.VMEM((rows, 1), f32),
            pltpu.VMEM((3, count, rows), b16),
            pltpu.VMEM((2, count, 1), f32),
            dma((4,)),
            dma((2,)),
        ]
        + [dma((2, steps))] * 11,
        compiler_params=pltpu.CompilerParams(
            collective_id=0, has_side_effects=True, vmem_limit_bytes=62 << 20
        ),
        cost_estimate=pl.CostEstimate(
            flops=16 * rows * model * half, bytes_accessed=60_000_000, transcendentals=4 * rows * half
        ),
    )(
        rising_ids[0].T,
        rising_gates[0].T,
        rising_drop[0],
        sinking_ids[0].T,
        sinking_gates[0].T,
        sinking_drop[0],
        rising_in[0],
        sinking_grad[0],
        sinking_pre.reshape(owners, pairs, cap, half),
        w_in[0, 0],
        w_out[0, 0],
    )
    return (result[0][None], result[1][None])


def solution(mesh):
    placed = (
        P("pipe", ("expert", "dp"), None),
        P("pipe", ("expert", "dp"), None),
        P("pipe", ("expert", "dp"), None),
        P("pipe", None, ("expert", "dp")),
        P("pipe", ("expert", "dp"), None),
        P("pipe", ("expert", "dp"), None),
        P("pipe", ("expert", "dp"), None),
        P("pipe", None, ("expert", "dp")),
        P("pipe", "expert", None, "dp"),
        P("pipe", "expert", None, "dp"),
        P("pipe", "expert", "dp", None),
    )
    return jax.shard_map(
        local,
        mesh=mesh,
        in_specs=placed,
        out_specs=(P("pipe", ("expert", "dp"), None), P("pipe", ("expert", "dp"), None)),
        check_vma=False,
    )
```

```python
import functools

import jax
import jax.experimental.pallas as pl
import jax.experimental.pallas.tpu as pltpu
import jax.numpy as jnp
from jax import lax
from jax.sharding import PartitionSpec as P

keep_scale = 1.0 / 0.9
root_half = 0.7071067811865476
inv_root_tau = 0.3989422804014327
MESH = pl.DeviceIdType.MESH
CHUNK = 512
CUTS = 2
LAG = 3


def gelu_value(h):
    return h * (0.5 * (1.0 + lax.erf(h * root_half)))


def gelu_slope(h):
    return 0.5 * (1.0 + lax.erf(h * root_half)) + h * inv_root_tau * jnp.exp(-0.5 * h * h)


def coefficients(words, gates):
    lanes = lax.broadcasted_iota(jnp.int32, gates.shape, 1)
    word = jnp.zeros(gates.shape, jnp.int32)
    for q in range(words.shape[1]):
        word = jnp.where(lanes // 32 == q, words[:, q : q + 1], word)
    keep = (jnp.right_shift(word, lanes % 32) & 1).astype(jnp.float32)
    return keep * gates * keep_scale


def routing(ids, owners, cap):
    top, count = ids.shape
    names = lax.broadcasted_iota(jnp.int32, (owners, count), 0)
    named = [ids[k : k + 1, :] == names for k in range(top)]
    hit = jnp.where(jnp.logical_or(named[0], named[1]), 1.0, 0.0)
    upto = lax.broadcasted_iota(jnp.int32, (count, count), 0) <= lax.broadcasted_iota(
        jnp.int32, (count, count), 1
    )
    place = jnp.dot(hit, jnp.where(upto, 1.0, 0.0), preferred_element_type=jnp.float32)
    row = place - 1.0 + (names * cap).astype(jnp.float32)
    return [jnp.sum(jnp.where(n, row, 0.0), axis=0, keepdims=True) for n in named]


def upright(row):
    n = row.shape[1]
    same = lax.broadcasted_iota(jnp.int32, (n, n), 0) == lax.broadcasted_iota(jnp.int32, (n, n), 1)
    return jnp.sum(jnp.where(same, row, 0.0), axis=1, keepdims=True)


def relay(
    sizes,
    ids_one, gates_one, drop_one, ids_two, gates_two, drop_two,
    rows_one, rows_two, saved, w_in, w_out,
    out_one, out_two,
    wi, wo, got_one, got_two, other_one, other_two, back_one, back_two,
    acc, act, pre, metas, zeros, staged, put, scale, hot, coef,
    load_sem, meta_sem, d_send, d_recv, s_send, s_recv, x_send, x_recv, c_send, c_recv,
    o_send, o_recv, l_sem,
):
    owners, cap, steps, width, sections = sizes
    rows = owners * cap
    p, me, core = lax.axis_index("pipe"), lax.axis_index("expert"), lax.axis_index("dp")
    odd = lax.rem(p, 2)
    across = p + 1 - 2 * odd
    sends_on = jnp.logical_and(odd == 0, p + 2 < sections)
    gets_on = jnp.logical_and(odd == 0, p >= 2)

    barrier = pltpu.get_barrier_semaphore()
    for d in range(1, owners):
        pl.semaphore_signal(
            barrier, device_id=(p, lax.rem(me + d, owners), core), device_id_type=MESH
        )
    for d in range(owners):
        pl.semaphore_signal(
            barrier, device_id=(across, lax.rem(me + d, owners), core), device_id_type=MESH
        )
    pl.semaphore_signal(barrier, device_id=(p, me, 1 - core), device_id_type=MESH)

    @pl.when(gets_on)
    def _():
        pl.semaphore_signal(barrier, device_id=(p - 2, me, core), device_id_type=MESH)

    load_in = pltpu.make_async_copy(w_in, wi, load_sem.at[0])
    load_out = pltpu.make_async_copy(w_out, wo, load_sem.at[1])
    load_pre = [
        pltpu.make_async_copy(saved.at[:, core if side == 0 else 1 - core], pre.at[side], load_sem.at[2 + side])
        for side in range(2)
    ]
    tokens = (rows_one, rows_two)

    def columns(j):
        return pl.ds(pl.multiple_of(j * width, width), width)

    def load_rows(m, j):
        return pltpu.make_async_copy(tokens[m].at[:, columns(j)], staged.at[m, j], l_sem.at[m, j])

    def loop(body):
        lax.fori_loop(0, steps, lambda j, _: (body(j), 0)[1], 0)

    loop(lambda j: load_rows(0, j).start())

    count = metas.shape[2]
    places = lax.broadcasted_iota(jnp.int32, (rows, count), 0).astype(jnp.float32)

    def place_rows(m, ids, gates, words):
        seats = routing(ids[...], owners, cap)
        mine = [places == seat for seat in seats]
        put[m] = jnp.where(jnp.logical_or(mine[0], mine[1]), 1.0, 0.0).astype(jnp.bfloat16)
        weights = coefficients(words[...], gates[...])
        for k in range(2):
            metas[0, 4 * m + k : 4 * m + k + 1, :] = seats[k]
        metas[0, 4 * m + 2 : 4 * m + 4, :] = weights
        if m == 1:
            scale[...] = jnp.sum(
                jnp.where(mine[0], weights[0:1], 0.0) + jnp.where(mine[1], weights[1:2], 0.0),
                axis=1, keepdims=True,
            )

    place_rows(0, ids_one, gates_one, drop_one)
    pl.semaphore_wait(barrier, 2 * owners + jnp.where(sends_on, 1, 0))

    gots, others = (got_one, got_two), (other_one, other_two)
    backs, outs = (back_one, back_two), (out_one, out_two)

    def dispatch(m, j):
        load_rows(m, j).wait()
        picked = jnp.dot(put[m], staged[m, j], preferred_element_type=jnp.float32)
        if m == 1:
            picked = scale[...] * picked
        others[m][j] = picked.reshape(owners, cap, width).astype(jnp.bfloat16)
        for d in range(1, owners):
            to = lax.rem(me + d, owners)
            pltpu.make_async_remote_copy(
                others[m].at[j, to], gots[m].at[j, 0, me],
                d_send.at[m, j], d_recv.at[m, j],
                device_id=(p, to, core), device_id_type=MESH,
            ).start()
        pltpu.make_async_copy(
            others[m].at[j, me], gots[m].at[j, 0, me], d_recv.at[m, j]
        ).start()

    def swap(m, j):
        return pltpu.make_async_remote_copy(
            gots[m].at[j, 0], gots[m].at[j, 1], s_send.at[m, j], s_recv.at[m, j],
            device_id=(p, me, 1 - core), device_id_type=MESH,
        )

    def cross(m, j):
        return pltpu.make_async_remote_copy(
            gots[m].at[j, 1], others[m].at[j], x_send.at[m, j], x_recv.at[m, j],
            device_id=(p, me, 1 - core), device_id_type=MESH,
        )

    def whole(ref, sem):
        return pltpu.make_async_copy(ref, ref, sem)

    def flat(ref):
        return ref[...].reshape(rows, width)

    def receive(m, j):
        whole(others[m].at[j, pl.ds(0, owners - 1)], d_send.at[m, j]).wait()
        whole(gots[m].at[j, 0], d_recv.at[m, j]).wait()
        swap(m, j).start()
        for side in range(2):
            if side == 1:
                swap(m, j).wait()
            block = flat(gots[m].at[j, side])
            if m == 0:
                acc[m, side] += jnp.dot(
                    block, wi[columns(j), :], preferred_element_type=jnp.float32
                )
            else:
                acc[m, side] += lax.dot_general(
                    block, wo[:, columns(j)], (((1,), (1,)), ((), ())),
                    preferred_element_type=jnp.float32,
                )

    def project(m, j, side):
        if m == 0:
            part = jnp.dot(act[m, side], wo[:, columns(j)], preferred_element_type=jnp.float32)
        else:
            part = lax.dot_general(
                act[m, side], wi[columns(j), :], (((1,), (1,)), ((), ())),
                preferred_element_type=jnp.float32,
            )
        return part.reshape(owners, cap, width).astype(jnp.bfloat16)

    def piece(h):
        return slice(h * width // CUTS, (h + 1) * width // CUTS)

    def send_back(m, j, s, at):
        for d in range(owners):
            to = lax.rem(me + d, owners)
            pltpu.make_async_remote_copy(
                gots[m].at[j, 0, to, :, at], backs[m].at[j, me, :, at],
                c_send.at[m, s], c_recv.at[m, s],
                device_id=(across, to, core), device_id_type=MESH,
            ).start()

    def give_back(m, j, cut=False):
        gots[m][j, 1] = project(m, j, 1)
        cross(m, j).start()
        part = project(m, j, 0)
        cross(m, j).wait()
        gots[m][j, 0] = (
            part.astype(jnp.float32) + others[m][j].astype(jnp.float32)
        ).astype(jnp.bfloat16)
        if cut:
            for h in range(CUTS):
                send_back(m, j, j + h, piece(h))
        else:
            send_back(m, j, j, slice(None))

    def place(m, j, at):
        size = len(range(*at.indices(width)))
        return outs[m].at[:, pl.ds(pl.multiple_of(j * width + (at.start or 0), size), size)]

    def out_local(m, j, s, at):
        return pltpu.make_async_copy(staged.at[m, j, :, at], place(m, j, at), o_send.at[m, s])

    def out_zero(m, j, s, at):
        return pltpu.make_async_copy(zeros.at[:, at], place(m, j, at), o_recv.at[m, s])

    def out_on(m, j, s, at):
        return pltpu.make_async_remote_copy(
            staged.at[m, j, :, at], place(m, j, at), o_send.at[m, s], o_recv.at[m, s],
            device_id=(lax.rem(p + 2, sections), me, core), device_id_type=MESH,
        )

    def collect(m, j, s=None, at=slice(None)):
        s = j if s is None else s
        whole(backs[m].at[j, :, :, at], c_recv.at[m, s]).wait()
        block = backs[m][j, :, :, at].reshape(rows, -1)

        def rows_of(n):
            return jnp.dot(hot[n], block, preferred_element_type=jnp.float32)

        if m == 0:
            total = coef[0] * rows_of(0) + coef[1] * rows_of(1)
        else:
            total = rows_of(2)
        staged[m, j, :, at] = total.astype(jnp.bfloat16)

        @pl.when(odd == 1)
        def _():
            out_local(m, j, s, at).start()

        @pl.when(sends_on)
        def _():
            out_on(m, j, s, at).start()

        @pl.when(p == 0)
        def _():
            out_zero(m, j, s, at).start()

    meta_far = pltpu.make_async_remote_copy(
        metas.at[0], metas.at[1], meta_sem.at[0], meta_sem.at[1],
        device_id=(across, me, core), device_id_type=MESH,
    )
    dispatch(0, 0)
    load_in.start()
    loop(lambda j: load_rows(1, j).start())
    load_out.start()
    for copy in load_pre:
        copy.start()
    lax.fori_loop(1, steps, lambda j, _: (dispatch(0, j), 0)[1], 0)
    place_rows(1, ids_two, gates_two, drop_two)
    zeros[...] = jnp.zeros_like(zeros)
    meta_far.start()
    acc[...] = jnp.zeros_like(acc)
    load_in.wait()

    def first(j):
        dispatch(1, j)
        receive(0, j)

    loop(first)
    for side in range(2):
        act[0, side] = gelu_value(acc[0, side]).astype(jnp.bfloat16)
    load_out.wait()

    def second(j):
        give_back(0, j)
        receive(1, j)

    loop(second)
    for copy in load_pre:
        copy.wait()
    for side in range(2):
        slope = gelu_slope(pre[side].astype(jnp.float32)).reshape(rows, pre.shape[3])
        act[1, side] = (acc[1, side] * slope).astype(jnp.bfloat16)
    meta_far.wait()
    seat_at = lax.broadcasted_iota(jnp.int32, (count, rows), 1).astype(jnp.float32)

    def theirs(n):
        return seat_at == upright(metas[1, n : n + 1, :])

    for k in range(2):
        hot[k] = jnp.where(theirs(k), 1.0, 0.0).astype(jnp.bfloat16)
        coef[k] = upright(metas[1, 2 + k : 3 + k, :])
    hot[2] = jnp.where(jnp.logical_or(theirs(4), theirs(5)), 1.0, 0.0).astype(jnp.bfloat16)

    def third(j):
        give_back(1, j)
        collect(0, j)

    last = steps - 1
    lax.fori_loop(0, last, lambda j, _: (third(j), 0)[1], 0)
    give_back(1, last, True)
    collect(0, last)
    def drain(m, j, s, at):
        whole(gots[m].at[j, 0, :, :, at], c_send.at[m, s]).wait()

        @pl.when(odd == 1)
        def _():
            out_local(m, j, s, at).wait()

        @pl.when(sends_on)
        def _():
            out_on(m, j, s, at).wait_send()

        @pl.when(gets_on)
        def _():
            out_on(m, j, s, at).wait_recv()

        @pl.when(p == 0)
        def _():
            out_zero(m, j, s, at).wait()

    def fourth(j):
        collect(1, j)
        drain(0, j, j, slice(None))

        @pl.when(j >= LAG)
        def _():
            drain(1, j - LAG, j - LAG, slice(None))

    lax.fori_loop(0, last, lambda j, _: (fourth(j), 0)[1], 0)
    drain(0, last, last, slice(None))
    for h in range(CUTS):
        collect(1, last, last + h, piece(h))
    for j in range(last - LAG, last):
        drain(1, j, j, slice(None))
    for h in range(CUTS):
        drain(1, last, last + h, piece(h))


def move(one, two, out_one, out_two, held, sem_in, sem_out):
    part = one.shape[0] // 4
    pieces = [
        (n, i, pl.ds(i * part, part), refs)
        for n, refs in enumerate(((one, out_one), (two, out_two)))
        for i in range(4)
    ]
    loads = [
        pltpu.make_async_copy(a.at[at], held.at[n, at], sem_in.at[n, i])
        for n, i, at, (a, _) in pieces
    ]
    stores = [
        pltpu.make_async_copy(held.at[n, at], b.at[at], sem_out.at[n, i])
        for n, i, at, (_, b) in pieces
    ]
    for copy in loads:
        copy.start()
    for load, store in zip(loads, stores):
        load.wait()
        store.start()
    for copy in stores:
        copy.wait()


def local(
    rising_in,
    rising_ids,
    rising_gates,
    rising_drop,
    sinking_grad,
    sinking_ids,
    sinking_gates,
    sinking_drop,
    sinking_pre,
    w_in,
    w_out,
):
    owners, pairs, sections = lax.axis_size("expert"), lax.axis_size("dp"), lax.axis_size("pipe")
    slots, half = sinking_pre.shape[2:]
    count, model = rising_in.shape[1:]
    cap = slots // (owners * pairs)
    rows = owners * cap
    width = CHUNK
    steps = model // width
    hbm = pl.BlockSpec(memory_space=pl.ANY)
    b16, f32 = jnp.bfloat16, jnp.float32
    dma = pltpu.SemaphoreType.DMA
    result = pl.pallas_call(
        functools.partial(relay, (owners, cap, steps, width, sections)),
        out_shape=(
            jax.ShapeDtypeStruct((count, model), b16),
            jax.ShapeDtypeStruct((count, model), b16),
        ),
        in_specs=[pl.BlockSpec(memory_space=pltpu.VMEM)] * 6 + [hbm] * 5,
        out_specs=(hbm,) * 2,
        scratch_shapes=[
            pltpu.VMEM((model, half), b16),
            pltpu.VMEM((half, model), b16),
            pltpu.VMEM((steps, 2, owners, cap, width), b16),
            pltpu.VMEM((steps, 2, owners, cap, width), b16),
            pltpu.VMEM((steps, owners, cap, width), b16),
            pltpu.VMEM((steps, owners, cap, width), b16),
            pltpu.VMEM((steps, owners, cap, width), b16),
            pltpu.VMEM((steps, owners, cap, width), b16),
            pltpu.VMEM((2, 2, rows, half), f32),
            pltpu.VMEM((2, 2, rows, half), b16),
            pltpu.VMEM((2, owners, cap, half), b16),
            pltpu.VMEM((2, 8, count), f32),
            pltpu.VMEM((count, width), b16),
            pltpu.VMEM((2, steps, count, width), b16),
            pltpu.VMEM((2, rows, count), b16),
            pltpu.VMEM((rows, 1), f32),
            pltpu.VMEM((3, count, rows), b16),
            pltpu.VMEM((2, count, 1), f32),
            dma((4,)),
            dma((2,)),
        ]
        + [dma((2, steps + CUTS))] * 11,
        compiler_params=pltpu.CompilerParams(
            collective_id=0, has_side_effects=True, vmem_limit_bytes=62 << 20
        ),
        cost_estimate=pl.CostEstimate(
            flops=16 * rows * model * half, bytes_accessed=60_000_000, transcendentals=4 * rows * half
        ),
    )(
        rising_ids[0].T,
        rising_gates[0].T,
        rising_drop[0],
        sinking_ids[0].T,
        sinking_gates[0].T,
        sinking_drop[0],
        rising_in[0],
        sinking_grad[0],
        sinking_pre.reshape(owners, pairs, cap, half),
        w_in[0, 0],
        w_out[0, 0],
    )
    result = pl.pallas_call(
        move,
        out_shape=(jax.ShapeDtypeStruct((count, model), b16),) * 2,
        in_specs=[hbm] * 2,
        out_specs=(hbm,) * 2,
        scratch_shapes=[pltpu.VMEM((2, count, model), b16), dma((2, 4)), dma((2, 4))],
    )(*result)
    return (result[0][None], result[1][None])


def solution(mesh):
    placed = (
        P("pipe", ("expert", "dp"), None),
        P("pipe", ("expert", "dp"), None),
        P("pipe", ("expert", "dp"), None),
        P("pipe", None, ("expert", "dp")),
        P("pipe", ("expert", "dp"), None),
        P("pipe", ("expert", "dp"), None),
        P("pipe", ("expert", "dp"), None),
        P("pipe", None, ("expert", "dp")),
        P("pipe", "expert", None, "dp"),
        P("pipe", "expert", None, "dp"),
        P("pipe", "expert", "dp", None),
    )
    return jax.shard_map(
        local,
        mesh=mesh,
        in_specs=placed,
        out_specs=(P("pipe", ("expert", "dp"), None), P("pipe", ("expert", "dp"), None)),
        check_vma=False,
    )
```

```python
import functools

import jax
import jax.experimental.pallas as pl
import jax.experimental.pallas.tpu as pltpu
import jax.numpy as jnp
from jax import lax
from jax.sharding import PartitionSpec as P

keep_scale = 1.0 / 0.9
root_half = 0.7071067811865476
inv_root_tau = 0.3989422804014327
MESH = pl.DeviceIdType.MESH
CHUNK = 512
CUTS = 2
LAG = 3
DIRECT = 1


def gelu_value(h):
    return h * (0.5 * (1.0 + lax.erf(h * root_half)))


def gelu_slope(h):
    return 0.5 * (1.0 + lax.erf(h * root_half)) + h * inv_root_tau * jnp.exp(-0.5 * h * h)


def coefficients(words, gates):
    lanes = lax.broadcasted_iota(jnp.int32, gates.shape, 1)
    word = jnp.zeros(gates.shape, jnp.int32)
    for q in range(words.shape[1]):
        word = jnp.where(lanes // 32 == q, words[:, q : q + 1], word)
    keep = (jnp.right_shift(word, lanes % 32) & 1).astype(jnp.float32)
    return keep * gates * keep_scale


def routing(ids, owners, cap):
    top, count = ids.shape
    names = lax.broadcasted_iota(jnp.int32, (owners, count), 0)
    named = [ids[k : k + 1, :] == names for k in range(top)]
    hit = jnp.where(jnp.logical_or(named[0], named[1]), 1.0, 0.0)
    upto = lax.broadcasted_iota(jnp.int32, (count, count), 0) <= lax.broadcasted_iota(
        jnp.int32, (count, count), 1
    )
    place = jnp.dot(hit, jnp.where(upto, 1.0, 0.0), preferred_element_type=jnp.float32)
    row = place - 1.0 + (names * cap).astype(jnp.float32)
    return [jnp.sum(jnp.where(n, row, 0.0), axis=0, keepdims=True) for n in named]


def upright(row):
    n = row.shape[1]
    same = lax.broadcasted_iota(jnp.int32, (n, n), 0) == lax.broadcasted_iota(jnp.int32, (n, n), 1)
    return jnp.sum(jnp.where(same, row, 0.0), axis=1, keepdims=True)


def relay(
    sizes,
    ids_one, gates_one, drop_one, ids_two, gates_two, drop_two,
    rows_one, rows_two, saved, w_in, w_out,
    out_one, out_two,
    wi, wo, got_one, got_two, other_one, other_two, back_one, back_two,
    acc, act, pre, metas, zeros, staged, put, scale, hot, coef,
    load_sem, meta_sem, d_send, d_recv, s_send, s_recv, x_send, x_recv, c_send, c_recv,
    o_send, o_recv, l_sem,
):
    owners, cap, steps, width, sections = sizes
    rows = owners * cap
    p, me, core = lax.axis_index("pipe"), lax.axis_index("expert"), lax.axis_index("dp")
    odd = lax.rem(p, 2)
    across = p + 1 - 2 * odd
    onward = lax.rem(p + 1, sections)
    has_next, has_prior = p + 1 < sections, p >= 1
    sends_on = jnp.logical_and(odd == 0, p + 2 < sections)
    gets_on = jnp.logical_and(odd == 0, p >= 2)

    barrier = pltpu.get_barrier_semaphore()
    for d in range(1, owners):
        pl.semaphore_signal(
            barrier, device_id=(p, lax.rem(me + d, owners), core), device_id_type=MESH
        )
    for d in range(owners):
        pl.semaphore_signal(
            barrier, device_id=(across, lax.rem(me + d, owners), core), device_id_type=MESH
        )
    pl.semaphore_signal(barrier, device_id=(p, me, 1 - core), device_id_type=MESH)

    @pl.when(gets_on)
    def _():
        pl.semaphore_signal(barrier, device_id=(p - 2, me, core), device_id_type=MESH)
        for d in range(owners):
            pl.semaphore_signal(
                barrier, device_id=(p - 1, lax.rem(me + d, owners), core), device_id_type=MESH
            )

    load_in = pltpu.make_async_copy(w_in, wi, load_sem.at[0])
    load_out = pltpu.make_async_copy(w_out, wo, load_sem.at[1])
    load_pre = [
        pltpu.make_async_copy(saved.at[:, core if side == 0 else 1 - core], pre.at[side], load_sem.at[2 + side])
        for side in range(2)
    ]
    tokens = (rows_one, rows_two)

    def columns(j):
        return pl.ds(pl.multiple_of(j * width, width), width)

    def load_rows(m, j):
        return pltpu.make_async_copy(tokens[m].at[:, columns(j)], staged.at[m, j], l_sem.at[m, j])

    def loop(body):
        lax.fori_loop(0, steps, lambda j, _: (body(j), 0)[1], 0)

    loop(lambda j: load_rows(0, j).start())

    count = metas.shape[2]
    places = lax.broadcasted_iota(jnp.int32, (rows, count), 0).astype(jnp.float32)

    def place_rows(m, ids, gates, words):
        seats = routing(ids[...], owners, cap)
        mine = [places == seat for seat in seats]
        put[m] = jnp.where(jnp.logical_or(mine[0], mine[1]), 1.0, 0.0).astype(jnp.bfloat16)
        weights = coefficients(words[...], gates[...])
        for k in range(2):
            metas[0, 4 * m + k : 4 * m + k + 1, :] = seats[k]
        metas[0, 4 * m + 2 : 4 * m + 4, :] = weights
        if m == 1:
            scale[...] = jnp.sum(
                jnp.where(mine[0], weights[0:1], 0.0) + jnp.where(mine[1], weights[1:2], 0.0),
                axis=1, keepdims=True,
            )

    place_rows(0, ids_one, gates_one, drop_one)
    pl.semaphore_wait(
        barrier,
        2 * owners
        + jnp.where(sends_on, 1, 0)
        + jnp.where(jnp.logical_and(odd == 1, has_next), owners, 0),
    )

    gots, others = (got_one, got_two), (other_one, other_two)
    backs, outs = (back_one, back_two), (out_one, out_two)

    def dispatch(m, j):
        load_rows(m, j).wait()
        picked = jnp.dot(put[m], staged[m, j], preferred_element_type=jnp.float32)
        if m == 1:
            picked = scale[...] * picked
        others[m][j] = picked.reshape(owners, cap, width).astype(jnp.bfloat16)
        for d in range(1, owners):
            to = lax.rem(me + d, owners)
            pltpu.make_async_remote_copy(
                others[m].at[j, to], gots[m].at[j, 0, me],
                d_send.at[m, j], d_recv.at[m, j],
                device_id=(p, to, core), device_id_type=MESH,
            ).start()
        pltpu.make_async_copy(
            others[m].at[j, me], gots[m].at[j, 0, me], d_recv.at[m, j]
        ).start()

    def swap(m, j):
        return pltpu.make_async_remote_copy(
            gots[m].at[j, 0], gots[m].at[j, 1], s_send.at[m, j], s_recv.at[m, j],
            device_id=(p, me, 1 - core), device_id_type=MESH,
        )

    def cross(m, j):
        return pltpu.make_async_remote_copy(
            gots[m].at[j, 1], others[m].at[j], x_send.at[m, j], x_recv.at[m, j],
            device_id=(p, me, 1 - core), device_id_type=MESH,
        )

    def whole(ref, sem):
        return pltpu.make_async_copy(ref, ref, sem)

    def flat(ref):
        return ref[...].reshape(rows, width)

    def receive(m, j):
        whole(others[m].at[j, pl.ds(0, owners - 1)], d_send.at[m, j]).wait()
        whole(gots[m].at[j, 0], d_recv.at[m, j]).wait()
        swap(m, j).start()
        for side in range(2):
            if side == 1:
                swap(m, j).wait()
            block = flat(gots[m].at[j, side])
            if m == 0:
                acc[m, side] += jnp.dot(
                    block, wi[columns(j), :], preferred_element_type=jnp.float32
                )
            else:
                acc[m, side] += lax.dot_general(
                    block, wo[:, columns(j)], (((1,), (1,)), ((), ())),
                    preferred_element_type=jnp.float32,
                )

    def project(m, j, side):
        if m == 0:
            part = jnp.dot(act[m, side], wo[:, columns(j)], preferred_element_type=jnp.float32)
        else:
            part = lax.dot_general(
                act[m, side], wi[columns(j), :], (((1,), (1,)), ((), ())),
                preferred_element_type=jnp.float32,
            )
        return part.reshape(owners, cap, width).astype(jnp.bfloat16)

    def piece(h):
        return slice(h * width // CUTS, (h + 1) * width // CUTS)

    def send_back(m, j, s, at, section=None):
        for d in range(owners):
            to = lax.rem(me + d, owners)
            pltpu.make_async_remote_copy(
                gots[m].at[j, 0, to, :, at], backs[m].at[j, me, :, at],
                c_send.at[m, s], c_recv.at[m, s],
                device_id=(across if section is None else section, to, core), device_id_type=MESH,
            ).start()

    def give_back(m, j, cut=False):
        gots[m][j, 1] = project(m, j, 1)
        cross(m, j).start()
        part = project(m, j, 0)
        cross(m, j).wait()
        gots[m][j, 0] = (
            part.astype(jnp.float32) + others[m][j].astype(jnp.float32)
        ).astype(jnp.bfloat16)
        if cut:
            for h in range(CUTS):
                if h < DIRECT:
                    send_back(m, j, j + h, piece(h))
                else:

                    @pl.when(has_next)
                    def _():
                        send_back(m, j, j + h, piece(h), onward)
        else:
            send_back(m, j, j, slice(None))

    def place(m, j, at):
        size = len(range(*at.indices(width)))
        return outs[m].at[:, pl.ds(pl.multiple_of(j * width + (at.start or 0), size), size)]

    def out_local(m, j, s, at):
        return pltpu.make_async_copy(staged.at[m, j, :, at], place(m, j, at), o_send.at[m, s])

    def out_zero(m, j, s, at):
        return pltpu.make_async_copy(zeros.at[:, at], place(m, j, at), o_recv.at[m, s])

    def out_on(m, j, s, at):
        return pltpu.make_async_remote_copy(
            staged.at[m, j, :, at], place(m, j, at), o_send.at[m, s], o_recv.at[m, s],
            device_id=(lax.rem(p + 2, sections), me, core), device_id_type=MESH,
        )

    def collect_direct(m, j, s, at):
        @pl.when(has_prior)
        def _():
            whole(backs[m].at[j, :, :, at], c_recv.at[m, s]).wait()
            block = backs[m][j, :, :, at].reshape(rows, -1)
            total = jnp.dot(hot[3], block, preferred_element_type=jnp.float32)
            staged[m, j, :, at] = total.astype(jnp.bfloat16)
            out_local(m, j, s, at).start()

        @pl.when(p == 0)
        def _():
            out_zero(m, j, s, at).start()

    def drain_direct(m, j, s, at):
        @pl.when(has_next)
        def _():
            whole(gots[m].at[j, 0, :, :, at], c_send.at[m, s]).wait()

        @pl.when(has_prior)
        def _():
            out_local(m, j, s, at).wait()

        @pl.when(p == 0)
        def _():
            out_zero(m, j, s, at).wait()

    def collect(m, j, s=None, at=slice(None)):
        s = j if s is None else s
        whole(backs[m].at[j, :, :, at], c_recv.at[m, s]).wait()
        block = backs[m][j, :, :, at].reshape(rows, -1)

        def rows_of(n):
            return jnp.dot(hot[n], block, preferred_element_type=jnp.float32)

        if m == 0:
            total = coef[0] * rows_of(0) + coef[1] * rows_of(1)
        else:
            total = rows_of(2)
        staged[m, j, :, at] = total.astype(jnp.bfloat16)

        @pl.when(odd == 1)
        def _():
            out_local(m, j, s, at).start()

        @pl.when(sends_on)
        def _():
            out_on(m, j, s, at).start()

        @pl.when(p == 0)
        def _():
            out_zero(m, j, s, at).start()

    meta_far = pltpu.make_async_remote_copy(
        metas.at[0], metas.at[1], meta_sem.at[0], meta_sem.at[1],
        device_id=(across, me, core), device_id_type=MESH,
    )
    dispatch(0, 0)
    load_in.start()
    loop(lambda j: load_rows(1, j).start())
    load_out.start()
    for copy in load_pre:
        copy.start()
    lax.fori_loop(1, steps, lambda j, _: (dispatch(0, j), 0)[1], 0)
    place_rows(1, ids_two, gates_two, drop_two)
    zeros[...] = jnp.zeros_like(zeros)
    meta_far.start()
    meta_on = pltpu.make_async_remote_copy(
        metas.at[0], metas.at[2], meta_sem.at[2], meta_sem.at[3],
        device_id=(onward, me, core), device_id_type=MESH,
    )

    @pl.when(has_next)
    def _():
        meta_on.start()

    acc[...] = jnp.zeros_like(acc)
    load_in.wait()

    def first(j):
        dispatch(1, j)
        receive(0, j)

    loop(first)
    for side in range(2):
        act[0, side] = gelu_value(acc[0, side]).astype(jnp.bfloat16)
    load_out.wait()

    def second(j):
        give_back(0, j)
        receive(1, j)

    loop(second)
    for copy in load_pre:
        copy.wait()
    for side in range(2):
        slope = gelu_slope(pre[side].astype(jnp.float32)).reshape(rows, pre.shape[3])
        act[1, side] = (acc[1, side] * slope).astype(jnp.bfloat16)
    meta_far.wait()
    seat_at = lax.broadcasted_iota(jnp.int32, (count, rows), 1).astype(jnp.float32)

    def theirs(n, slot=1):
        return seat_at == upright(metas[slot, n : n + 1, :])

    for k in range(2):
        hot[k] = jnp.where(theirs(k), 1.0, 0.0).astype(jnp.bfloat16)
        coef[k] = upright(metas[1, 2 + k : 3 + k, :])
    hot[2] = jnp.where(jnp.logical_or(theirs(4), theirs(5)), 1.0, 0.0).astype(jnp.bfloat16)

    @pl.when(has_next)
    def _():
        meta_on.wait_send()

    @pl.when(has_prior)
    def _():
        meta_on.wait_recv()
        hot[3] = jnp.where(
            jnp.logical_or(theirs(4, 2), theirs(5, 2)), 1.0, 0.0
        ).astype(jnp.bfloat16)


    def third(j):
        give_back(1, j)
        collect(0, j)

    last = steps - 1
    lax.fori_loop(0, last, lambda j, _: (third(j), 0)[1], 0)
    give_back(1, last, True)
    collect(0, last)
    def drain(m, j, s, at):
        whole(gots[m].at[j, 0, :, :, at], c_send.at[m, s]).wait()

        @pl.when(odd == 1)
        def _():
            out_local(m, j, s, at).wait()

        @pl.when(sends_on)
        def _():
            out_on(m, j, s, at).wait_send()

        @pl.when(gets_on)
        def _():
            out_on(m, j, s, at).wait_recv()

        @pl.when(p == 0)
        def _():
            out_zero(m, j, s, at).wait()

    def fourth(j):
        collect(1, j)
        drain(0, j, j, slice(None))

        @pl.when(j >= LAG)
        def _():
            drain(1, j - LAG, j - LAG, slice(None))

    lax.fori_loop(0, last, lambda j, _: (fourth(j), 0)[1], 0)
    drain(0, last, last, slice(None))
    for h in range(CUTS):
        (collect if h < DIRECT else collect_direct)(1, last, last + h, piece(h))
    for j in range(last - LAG, last):
        drain(1, j, j, slice(None))
    for h in range(CUTS):
        (drain if h < DIRECT else drain_direct)(1, last, last + h, piece(h))


def move(one, two, out_one, out_two, held, sem_in, sem_out):
    part = one.shape[0] // 4
    pieces = [
        (n, i, pl.ds(i * part, part), refs)
        for n, refs in enumerate(((one, out_one), (two, out_two)))
        for i in range(4)
    ]
    loads = [
        pltpu.make_async_copy(a.at[at], held.at[n, at], sem_in.at[n, i])
        for n, i, at, (a, _) in pieces
    ]
    stores = [
        pltpu.make_async_copy(held.at[n, at], b.at[at], sem_out.at[n, i])
        for n, i, at, (_, b) in pieces
    ]
    for copy in loads:
        copy.start()
    for load, store in zip(loads, stores):
        load.wait()
        store.start()
    for copy in stores:
        copy.wait()


def local(
    rising_in,
    rising_ids,
    rising_gates,
    rising_drop,
    sinking_grad,
    sinking_ids,
    sinking_gates,
    sinking_drop,
    sinking_pre,
    w_in,
    w_out,
):
    owners, pairs, sections = lax.axis_size("expert"), lax.axis_size("dp"), lax.axis_size("pipe")
    slots, half = sinking_pre.shape[2:]
    count, model = rising_in.shape[1:]
    cap = slots // (owners * pairs)
    rows = owners * cap
    width = CHUNK
    steps = model // width
    hbm = pl.BlockSpec(memory_space=pl.ANY)
    b16, f32 = jnp.bfloat16, jnp.float32
    dma = pltpu.SemaphoreType.DMA
    result = pl.pallas_call(
        functools.partial(relay, (owners, cap, steps, width, sections)),
        out_shape=(
            jax.ShapeDtypeStruct((count, model), b16),
            jax.ShapeDtypeStruct((count, model), b16),
        ),
        in_specs=[pl.BlockSpec(memory_space=pltpu.VMEM)] * 6 + [hbm] * 5,
        out_specs=(hbm,) * 2,
        scratch_shapes=[
            pltpu.VMEM((model, half), b16),
            pltpu.VMEM((half, model), b16),
            pltpu.VMEM((steps, 2, owners, cap, width), b16),
            pltpu.VMEM((steps, 2, owners, cap, width), b16),
            pltpu.VMEM((steps, owners, cap, width), b16),
            pltpu.VMEM((steps, owners, cap, width), b16),
            pltpu.VMEM((steps, owners, cap, width), b16),
            pltpu.VMEM((steps, owners, cap, width), b16),
            pltpu.VMEM((2, 2, rows, half), f32),
            pltpu.VMEM((2, 2, rows, half), b16),
            pltpu.VMEM((2, owners, cap, half), b16),
            pltpu.VMEM((3, 8, count), f32),
            pltpu.VMEM((count, width), b16),
            pltpu.VMEM((2, steps, count, width), b16),
            pltpu.VMEM((2, rows, count), b16),
            pltpu.VMEM((rows, 1), f32),
            pltpu.VMEM((4, count, rows), b16),
            pltpu.VMEM((2, count, 1), f32),
            dma((4,)),
            dma((4,)),
        ]
        + [dma((2, steps + CUTS))] * 11,
        compiler_params=pltpu.CompilerParams(
            collective_id=0, has_side_effects=True, vmem_limit_bytes=62 << 20
        ),
        cost_estimate=pl.CostEstimate(
            flops=16 * rows * model * half, bytes_accessed=60_000_000, transcendentals=4 * rows * half
        ),
    )(
        rising_ids[0].T,
        rising_gates[0].T,
        rising_drop[0],
        sinking_ids[0].T,
        sinking_gates[0].T,
        sinking_drop[0],
        rising_in[0],
        sinking_grad[0],
        sinking_pre.reshape(owners, pairs, cap, half),
        w_in[0, 0],
        w_out[0, 0],
    )
    result = pl.pallas_call(
        move,
        out_shape=(jax.ShapeDtypeStruct((count, model), b16),) * 2,
        in_specs=[hbm] * 2,
        out_specs=(hbm,) * 2,
        scratch_shapes=[pltpu.VMEM((2, count, model), b16), dma((2, 4)), dma((2, 4))],
    )(*result)
    return (result[0][None], result[1][None])


def solution(mesh):
    placed = (
        P("pipe", ("expert", "dp"), None),
        P("pipe", ("expert", "dp"), None),
        P("pipe", ("expert", "dp"), None),
        P("pipe", None, ("expert", "dp")),
        P("pipe", ("expert", "dp"), None),
        P("pipe", ("expert", "dp"), None),
        P("pipe", ("expert", "dp"), None),
        P("pipe", None, ("expert", "dp")),
        P("pipe", "expert", None, "dp"),
        P("pipe", "expert", None, "dp"),
        P("pipe", "expert", "dp", None),
    )
    return jax.shard_map(
        local,
        mesh=mesh,
        in_specs=placed,
        out_specs=(P("pipe", ("expert", "dp"), None), P("pipe", ("expert", "dp"), None)),
        check_vma=False,
    )
```
